128 devices in a mesh: tensor: 16 (over x_lo, y, core), replica: 8 (over z, x_hi).
Axes of the slice: x: 4 (x_hi: 2, x_lo: 2; x = x_hi * 2 + x_lo), y: 4, z: 4, core: 2. Of those that a mesh axis runs over, the one named last changes fastest.
Arguments:
- tokens: bfloat16 [5120, 4096], P(('replica', 'tensor')), may hold values from -6 to 6
- cotangent: bfloat16 [5120, 14336], P('replica', 'tensor'), may hold values from -6 to 6
- weights: bfloat16 [4096, 2, 14336], P(None, None, 'tensor'), may hold values from -0.09375 to 0.09375
- scores: float32 [4096, 2, 14336], P('replica', None, 'tensor'), may hold values from -6 to 6
- tile_mask: int32 [32, 2, 112], P(None, None, 'tensor'), may hold values 0 or 1
Outputs:
- token_grad: bfloat16 [5120, 4096], P(('replica', 'tensor'))
- weight_grad: bfloat16 [4096, 2, 14336], P('replica', None, 'tensor')
- new_scores: float32 [4096, 2, 14336], P('replica', None, 'tensor')
The draws below stay inside these ranges and needn't reach their ends.
All inputs are finite; a program needn't handle non-finite values. No bound on the sum of `tile_mask` on one device may be relied on, other than what follows from the above.
Results may differ from the reference program's by a relative error of at most 0.023.
Values may be sent and summed in bfloat16 or wider, within the bound.
No kernel may reach another device: no remote copies, remote signals or barrier semaphores. Data moves between devices by JAX's collectives and lax.ppermute only.
A program may use at most 256 MiB of HBM per device.

```python
import math
import jax
import jax.numpy as jnp
from jax import lax

D = 4096
TILE = 128
TOK_REP = 640
FF = 14336
TOKENS = 5120
N_REPLICA = 8


def with_ends(entries, key, low, top_value):
    longest = entries.shape.index(max(entries.shape))
    spots = []
    for shift in (0, 1):
        where = [jax.random.randint(jax.random.fold_in(key, axis), (), 0, length) for axis, length in enumerate(entries.shape)]
        where[longest] = (where[longest] + shift) % entries.shape[longest]
        spots.append(tuple(where))
    return entries.at[spots[0]].set(low).at[spots[1]].set(top_value)


def raised(entries, stream_key, source, target, parts, factor):
    def block_of(position):
        return (jnp.arange(entries.shape[position]) // (entries.shape[position] // parts)).reshape((-1,) + (1,) * (entries.ndim - 1 - position))

    one_side = jax.random.permutation(stream_key, parts)[block_of(target)]
    second = (block_of(target) + parts // 2) % parts
    return jnp.where((block_of(source) == one_side) | (block_of(source) == second), factor * entries, entries)


def block_levels(stream_key, extent, pieces, least, high):
    level, own = 1.0, jax.random.fold_in(stream_key, 6)
    for axis_at, blocks in pieces:
        draws = jnp.exp(jax.random.uniform(jax.random.fold_in(own, axis_at), (blocks,), jnp.float32, least / len(pieces), high / len(pieces)))
        level = level * jnp.repeat(draws, extent[axis_at] // blocks).reshape([-1 if axis == axis_at else 1 for axis in range(len(extent))])
    return level


def bell_draw(stream_key, extent, deviation, limit, cuts=(), kind=jnp.bfloat16):
    factor_of = block_levels(stream_key, extent, cuts, -0.22, 0.18) if cuts else 1.0
    values = jax.random.normal(stream_key, extent, jnp.float32) * deviation * factor_of
    return jnp.minimum(jnp.maximum(values, -limit), limit).astype(kind)


def gaussian_with(key, extent, scale, reach, shards, heavy, dtype=jnp.bfloat16):
    values = scale * jax.random.normal(key, extent, jnp.float32)
    if shards:
        values = values * block_levels(key, extent, shards, -0.22, 0.18)
    return jnp.clip(raised(values, jax.random.fold_in(key, 3), *heavy), -reach, reach).astype(dtype)


def setup_inputs(seed: int = 0) -> dict:
    keys = jax.random.split(jax.random.key(seed), 6)
    return {
        "tokens": bell_draw(keys[0], (TOKENS, D), 1.0, 6.0, ((0, 128),)),
        "cotangent": gaussian_with(keys[1], (TOKENS, FF), 1.0, 6.0, ((0, 8), (1, 16)), (1, 0, 16, 2.0)),
        "weights": bell_draw(keys[2], (D, 2, FF), D ** -0.5, 0.09375, ((2, 16),)),
        "scores": bell_draw(keys[3], (D, 2, FF), 1.0, 6.0, ((0, 8), (2, 16)), jnp.float32),
        "tile_mask": with_ends((jax.random.randint(keys[4], (D // TILE, 2, FF // TILE), 0, 4) < 3).astype(jnp.int32), jax.random.fold_in(keys[4], 1), 0, 1),
    }


def expand_mask(tile_mask):
    tile_rows, pair, tile_cols = tile_mask.shape
    grown = jnp.broadcast_to(tile_mask[:, None, :, :, None], (tile_rows, TILE, pair, tile_cols, TILE))
    return grown.reshape(tile_rows * TILE, pair, tile_cols * TILE).astype(jnp.float32)

def reference(tokens, cotangent, weights, scores, tile_mask):
    keep = expand_mask(tile_mask)
    masked = (weights.astype(jnp.float32) * keep).astype(jnp.bfloat16)
    flat = masked.reshape(D, 2 * FF)
    projected = jnp.dot(tokens, flat, preferred_element_type=jnp.float32)
    gate = projected[:, :FF]
    up = projected[:, FF:]
    sigmoid_gate = jax.nn.sigmoid(gate)
    upstream = cotangent.astype(jnp.float32)
    gate_grad = (upstream * up * sigmoid_gate * (1.0 + gate * (1.0 - sigmoid_gate))).astype(jnp.bfloat16)
    up_grad = (upstream * gate * sigmoid_gate).astype(jnp.bfloat16)
    both_grads = jnp.concatenate([gate_grad, up_grad], axis=1)
    token_grad = lax.dot_general(both_grads, flat, (((1,), (1,)), ((), ())), preferred_element_type=jnp.float32).astype(jnp.bfloat16)
    token_blocks = tokens.reshape(N_REPLICA, TOK_REP, D)
    grad_blocks = both_grads.reshape(N_REPLICA, TOK_REP, 2 * FF)

    def accumulate(carry, pair):
        part = lax.dot_general(pair[0], pair[1], (((0,), (0,)), ((), ())), preferred_element_type=jnp.float32)
        rounded = lax.optimization_barrier(part.astype(jnp.bfloat16))
        return (carry + rounded.astype(jnp.float32), None)
    summed, unused = lax.scan(accumulate, jnp.zeros((D, 2 * FF), jnp.float32), (token_blocks, grad_blocks))
    total = (summed * (1.0 / math.sqrt(TOKENS))).reshape(D, 2, FF)
    weight_grad = (keep * total).astype(jnp.bfloat16)
    new_scores = scores - math.sqrt(D) * weights.astype(jnp.float32) * total
    return (token_grad, weight_grad, new_scores)
```

```python
import functools
import math

import jax
import jax.numpy as jnp
from jax import lax
from jax.experimental import pallas as pl
from jax.experimental.pallas import tpu as pltpu
from jax.sharding import PartitionSpec as P

TILE = 128
CHUNKS = (2, 2, 2, 1)
CORE_MAJOR = [[*range(0, 16, 2), *range(1, 16, 2)]]
STAGES = (
    (("x_hi", 0), ("rest", 0)),
    (("x_hi", 1), ("far", 0), ("token", 0)),
    (("x_hi", 2), ("near", 0), ("sum", 0), ("far", 1)),
    (("x_hi", 3), ("near", 1), ("far", 2), ("last", 0)),
    (("near", 2), ("far", 3), ("last", 1)),
    (("near", 3), ("last", 2)),
    (("last", 3),),
)
MIB = 1 << 20


def params(mib):
    return pltpu.CompilerParams(vmem_limit_bytes=mib * MIB)


SMALL = pl.CostEstimate(flops=1, bytes_accessed=1, transcendentals=0)


def over_core(v):
    return lax.ppermute(v, "tensor", [(i, i ^ 1) for i in range(16)])


def over_x_lo(v):
    return lax.ppermute(v, "tensor", [(i, i ^ 8) for i in range(16)])


def over_y(v, step):
    pairs = [(i, (i & 9) | (((i >> 1) + step) % 4) << 1) for i in range(16)]
    return lax.ppermute(v, "tensor", pairs)


def over_z(v, step):
    return lax.ppermute(v, "replica", [(i, (i + 2 * step) % 8) for i in range(8)])


def over_x_hi(v):
    return lax.ppermute(v, "replica", [(i, i ^ 1) for i in range(8)])


def after(value, *earlier):
    return lax.optimization_barrier((value, *earlier))[0]


def slot_of(where, dx, dy):
    x_lo = where[2] if dx == 0 else 1 - where[2]
    return x_lo * 4 + lax.rem(where[3] + dy, 4)


def place_body(slots, where, *refs):
    out_ref = refs[-1]
    for piece, group in zip(refs, slots):
        value = piece[...]
        for i, (dx, dy) in enumerate(group):
            out_ref[slot_of(where, dx, dy)] = value[i] if len(group) > 1 else value


def place(where, pieces, slots):
    rows, width = pieces[0].shape[-2:]
    cols = width // 2
    specs = [
        pl.BlockSpec((rows, cols), lambda i, where: (0, i))
        if piece.ndim == 2
        else pl.BlockSpec((piece.shape[0], rows, cols), lambda i, where: (0, 0, i))
        for piece in pieces
    ]
    return pl.pallas_call(
        functools.partial(place_body, slots),
        grid_spec=pltpu.PrefetchScalarGridSpec(
            num_scalar_prefetch=1,
            grid=(2,),
            in_specs=specs,
            out_specs=pl.BlockSpec((8, rows, cols), lambda i, where: (0, 0, i)),
        ),
        out_shape=jax.ShapeDtypeStruct((8, rows, width), jnp.bfloat16),
        compiler_params=params(56),
        cost_estimate=SMALL,
        name="place",
    )(where, *pieces).reshape(8 * rows, width)


def mask_body(tiles, units, begin, where, mask_ref, w_ref, *rest):
    out_ref = rest[-1]
    step = pl.program_id(0) + begin // (tiles * TILE)
    for t in range(tiles):
        rows = slice(t * TILE, (t + 1) * TILE)
        block = w_ref[rows].reshape(TILE, 2 * units * TILE)
        for j in range(units):
            for k in range(2):
                keep = mask_ref[step * tiles + t, k, j].astype(jnp.float32).astype(jnp.bfloat16)
                at = (k * units + j) * TILE
                out_ref[j, rows, k * TILE : (k + 1) * TILE] = block[:, at : at + TILE] * keep


def mask_weights(where, weights, tile_mask, begin, end, done):
    width, pair, hidden = weights.shape
    units = hidden // TILE
    rows = 256
    operands = [where, tile_mask, weights] + ([] if done is None else [done])
    return pl.pallas_call(
        functools.partial(mask_body, rows // TILE, units, begin),
        grid_spec=pltpu.PrefetchScalarGridSpec(
            num_scalar_prefetch=1,
            grid=((end - begin) // rows,),
            in_specs=[
                pl.BlockSpec(memory_space=pltpu.SMEM),
                pl.BlockSpec((rows, pair, hidden), lambda i, where: (i + begin // rows, 0, 0)),
            ]
            + ([] if done is None else [pl.BlockSpec(memory_space=pl.ANY)]),
            out_specs=pl.BlockSpec((units, rows, 256), lambda i, where: (0, i + begin // rows, 0)),
        ),
        out_shape=jax.ShapeDtypeStruct((units, width, 256), jnp.bfloat16),
        input_output_aliases={} if done is None else {3: 0},
        compiler_params=params(56),
        cost_estimate=SMALL,
        name="mask_weights",
    )(*operands)


def unit(tok, w, cot):
    both = jnp.dot(tok, w, preferred_element_type=jnp.float32)
    gate, up = both[:, :TILE], both[:, TILE:]
    sig = 1.0 / (1.0 + jnp.exp(-gate))
    upstream = cot.astype(jnp.float32)
    gate_grad = upstream * up * sig * (1.0 + gate * (1.0 - sig))
    return gate_grad.astype(jnp.bfloat16), (upstream * gate * sig).astype(jnp.bfloat16)


def first_body(where, mine_l, theirs_l, mine_r, theirs_r, w_ref, cot_ref, out_ref, tok_ref, held, sems):
    step = pl.program_id(0)
    saves = [pltpu.make_async_copy(held.at[i], tok_ref.at[i], sems.at[i]) for i in range(2)]

    @pl.when(step == 0)
    def _():
        core = where[4]
        half = mine_l.shape[1]
        left, right = pl.ds(0, half), pl.ds(half, half)
        loads = [
            pltpu.make_async_copy(mine_l, held.at[core, :, left], sems.at[0]),
            pltpu.make_async_copy(theirs_l, held.at[1 - core, :, left], sems.at[1]),
            pltpu.make_async_copy(mine_r, held.at[core, :, right], sems.at[2]),
            pltpu.make_async_copy(theirs_r, held.at[1 - core, :, right], sems.at[3]),
        ]
        for load in loads:
            load.start()
        for load in loads:
            load.wait()
        for save in saves:
            save.start()

    tok = held[...].reshape(2 * held.shape[1], held.shape[2])
    out_ref[0, :, :TILE], out_ref[0, :, TILE:] = unit(tok, w_ref[0], cot_ref[...])

    @pl.when(step == pl.num_programs(0) - 1)
    def _():
        for save in saves:
            save.wait()


def first_grads(where, parts, masked, cot, count):
    rows, width = parts[0].shape[0], masked.shape[1]
    grads, tok = pl.pallas_call(
        first_body,
        grid_spec=pltpu.PrefetchScalarGridSpec(
            num_scalar_prefetch=1,
            grid=(count,),
            in_specs=[
                *[pl.BlockSpec(memory_space=pl.ANY)] * 4,
                pl.BlockSpec((1, width, 256), lambda j, where: (j, 0, 0)),
                pl.BlockSpec((2 * rows, TILE), lambda j, where: (0, j)),
            ],
            out_specs=[
                pl.BlockSpec((1, 2 * rows, 256), lambda j, where: (j, 0, 0)),
                pl.BlockSpec(memory_space=pl.ANY),
            ],
            scratch_shapes=[pltpu.VMEM((2, rows, width), jnp.bfloat16), pltpu.SemaphoreType.DMA((4,))],
        ),
        out_shape=[
            jax.ShapeDtypeStruct((count, 2 * rows, 256), jnp.bfloat16),
            jax.ShapeDtypeStruct((2, rows, width), jnp.bfloat16),
        ],
        compiler_params=params(56),
        cost_estimate=SMALL,
        name="first_grads",
    )(where, *parts, masked, cot)
    return grads, tok.reshape(2 * rows, width)


def rest_body(counts, where, tok_ref, w_ref, cot_ref, *out_refs):
    step = pl.program_id(0)
    gate_grad, up_grad = unit(tok_ref[...], w_ref[0], cot_ref[...])
    start = 0
    for count, out_ref in zip(counts, out_refs):

        @pl.when((step >= start) & (step < start + count))
        def _(out_ref=out_ref):
            out_ref[0, :, :TILE] = gate_grad
            out_ref[0, :, TILE:] = up_grad

        start += count


def rest_grads(where, tok, masked, cot, first, counts):
    rows, width = tok.shape
    n = sum(counts)
    outs, start = [], 0
    for count in counts:
        outs.append(
            pl.BlockSpec(
                (1, rows, 256),
                lambda j, where, s=start, c=count: (jnp.clip(j - s, 0, c - 1), 0, 0),
            )
        )
        start += count
    return pl.pallas_call(
        functools.partial(rest_body, counts),
        grid_spec=pltpu.PrefetchScalarGridSpec(
            num_scalar_prefetch=1,
            grid=(n,),
            in_specs=[
                pl.BlockSpec((rows, width), lambda j, where: (0, 0)),
                pl.BlockSpec((1, width, 256), lambda j, where: (j + first, 0, 0)),
                pl.BlockSpec((rows, TILE), lambda j, where: (0, j + first)),
            ],
            out_specs=outs,
        ),
        out_shape=[jax.ShapeDtypeStruct((c, rows, 256), jnp.bfloat16) for c in counts],
        compiler_params=params(56),
        cost_estimate=SMALL,
        name="rest_grads",
    )(where, tok, masked, cot)


def outer(tok_a, tok_b, g_a, g_b, j):
    dims = (((0,), (0,)), ((), ()))
    return lax.dot_general(
        tok_a[...], g_a[j], dims, preferred_element_type=jnp.float32
    ) + lax.dot_general(tok_b[...], g_b[j], dims, preferred_element_type=jnp.float32)


def far_body(count, where, tok_a, tok_b, g_a, g_b, up_ref, down_ref):
    for j in range(count):
        part = outer(tok_a, tok_b, g_a, g_b, j).astype(jnp.bfloat16)
        up_ref[j] = part[:256]
        down_ref[j] = part[256:]


def near_body(count, where, tok_ua, tok_ub, tok_da, tok_db, g_a, g_b, got_u, got_d, up_ref, down_ref):
    for j in range(count):
        part = outer(tok_ua, tok_ub, g_a, g_b, j)
        up_ref[j, :256] = (part[:256] + got_u[j].astype(jnp.float32)).astype(jnp.bfloat16)
        up_ref[j, 256:] = part[256:].astype(jnp.bfloat16)
        part = outer(tok_da, tok_db, g_a, g_b, j)
        down_ref[j, :256] = part[:256].astype(jnp.bfloat16)
        down_ref[j, 256:] = (part[256:] + got_d[j].astype(jnp.float32)).astype(jnp.bfloat16)


def last_body(
    count, first, scale, rate, where, mask_ref, tok_a, tok_b, g_a, g_b, got_u, got_d, w_ref, s_ref, *rest
):
    wg_ref, ns_ref = rest[-2:]
    row = (where[0] * 2 + where[1]) * 4
    side = lax.broadcasted_iota(jnp.int32, (1, 2, TILE), 1)
    for j in range(count):
        total = outer(tok_a, tok_b, g_a, g_b, j)
        total = total + got_u[j].astype(jnp.float32) + got_d[j].astype(jnp.float32)
        total = total * scale
        cols = slice(j * TILE, (j + 1) * TILE)
        for t in range(4):
            rows = slice(t * TILE, (t + 1) * TILE)
            keep = jnp.where(
                side == 0, mask_ref[row + t, 0, first + j], mask_ref[row + t, 1, first + j]
            ).astype(jnp.float32)
            here = total[rows].reshape(TILE, 2, TILE)
            wg_ref[rows, :, cols] = (here * keep).astype(jnp.bfloat16)
            ns_ref[rows, :, cols] = (
                s_ref[rows, :, cols] - rate * w_ref[rows, :, cols].astype(jnp.float32) * here
            )


def tok_spec(dz):
    return pl.BlockSpec((640, 512), lambda i, where: (0, 2 * ((where[0] + dz) % 4) + where[1]))


def other_spec(dz):
    return pl.BlockSpec((640, 512), lambda i, where: (0, (where[0] + dz) % 4))


def whole(shape):
    return pl.BlockSpec(shape, lambda i, where: (0,) * len(shape))


def far_rows(where, tok, tok_other, g, g_other):
    count = g.shape[0]
    shape = (count, 256, 256)
    return pl.pallas_call(
        functools.partial(far_body, count),
        grid_spec=pltpu.PrefetchScalarGridSpec(
            num_scalar_prefetch=1,
            grid=(1,),
            in_specs=[tok_spec(2), other_spec(2), whole(g.shape), whole(g.shape)],
            out_specs=[whole(shape)] * 2,
        ),
        out_shape=[jax.ShapeDtypeStruct(shape, jnp.bfloat16)] * 2,
        compiler_params=params(56),
        cost_estimate=SMALL,
        name="far_rows",
    )(where, tok, tok_other, g, g_other)


def near_rows(where, tok, tok_other, g, g_other, got_u, got_d):
    count = g.shape[0]
    shape = (count, 512, 256)
    return pl.pallas_call(
        functools.partial(near_body, count),
        grid_spec=pltpu.PrefetchScalarGridSpec(
            num_scalar_prefetch=1,
            grid=(1,),
            in_specs=[
                tok_spec(1),
                other_spec(1),
                tok_spec(3),
                other_spec(3),
                whole(g.shape),
                whole(g.shape),
                whole(got_u.shape),
                whole(got_d.shape),
            ],
            out_specs=[whole(shape)] * 2,
        ),
        out_shape=[jax.ShapeDtypeStruct(shape, jnp.bfloat16)] * 2,
        compiler_params=params(56),
        cost_estimate=SMALL,
        name="near_rows",
    )(where, tok, tok_other, tok, tok_other, g, g_other, got_u, got_d)


def last_rows(where, tile_mask, tok, tok_other, g, g_other, got_u, got_d, weights, scores, first, done, tokens):
    count = g.shape[0]
    n = count * TILE
    at = first // count
    specs = [
        pl.BlockSpec(memory_space=pltpu.SMEM),
        tok_spec(0),
        other_spec(0),
        whole(g.shape),
        whole(g.shape),
        whole(got_u.shape),
        whole(got_d.shape),
        pl.BlockSpec((512, 2, n), lambda i, where: (where[0] * 2 + where[1], 0, at)),
        pl.BlockSpec((512, 2, n), lambda i, where: (0, 0, at)),
    ]
    out = pl.BlockSpec((512, 2, n), lambda i, where: (0, 0, at))
    operands = [where, tile_mask, tok, tok_other, g, g_other, got_u, got_d, weights, scores]
    alias = {}
    if done is not None:
        alias = {len(operands): 0, len(operands) + 1: 1}
        specs += [pl.BlockSpec(memory_space=pl.ANY)] * 2
        operands += list(done)
    return pl.pallas_call(
        functools.partial(last_body, count, first, 1.0 / math.sqrt(tokens), math.sqrt(weights.shape[0])),
        grid_spec=pltpu.PrefetchScalarGridSpec(
            num_scalar_prefetch=1, grid=(1,), in_specs=specs, out_specs=[out, out]
        ),
        out_shape=[
            jax.ShapeDtypeStruct(scores.shape, jnp.bfloat16),
            jax.ShapeDtypeStruct(scores.shape, jnp.float32),
        ],
        input_output_aliases=alias,
        compiler_params=params(56),
        cost_estimate=SMALL,
        name="last_rows",
    )(*operands)


def token_body(parts, where, *refs):
    w_ref, out_ref = refs[parts:]
    total = None
    at = 0
    for g in refs[:parts]:
        for j in range(g.shape[0]):
            term = lax.dot_general(
                g[j], w_ref[at], (((1,), (1,)), ((), ())), preferred_element_type=jnp.float32
            )
            total = term if total is None else total + term
            at += 1
    rows = out_ref.shape[1]
    for i in range(8):
        for core in range(2):
            start = (core * 8 + i) * rows
            out_ref[i * 2 + core] = total[start : start + rows].astype(jnp.bfloat16)


def token_rows(where, gs, masked):
    units, width, unused = masked.shape
    rows, cols = gs[0].shape[1], 512
    specs = [pl.BlockSpec(g.shape, lambda i, where: (0, 0, 0)) for g in gs]
    specs.append(pl.BlockSpec((units, cols, 256), lambda i, where: (0, i, 0)))
    return pl.pallas_call(
        functools.partial(token_body, len(gs)),
        grid_spec=pltpu.PrefetchScalarGridSpec(
            num_scalar_prefetch=1,
            grid=(width // cols,),
            in_specs=specs,
            out_specs=pl.BlockSpec((16, rows // 16, cols), lambda i, where: (0, 0, i)),
        ),
        out_shape=jax.ShapeDtypeStruct((16, rows // 16, width), jnp.bfloat16),
        compiler_params=params(56),
        cost_estimate=SMALL,
        name="token_rows",
    )(where, *gs, masked).reshape(rows, width)


def shards(tokens, cotangent, weights, scores, tile_mask):
    place_at, replica = lax.axis_index("tensor"), lax.axis_index("replica")
    z, x_hi = replica // 2, replica % 2
    where = jnp.stack([z, x_hi, place_at // 8, (place_at // 2) % 4, place_at % 2]).astype(jnp.int32)
    rows, width = tokens.shape
    all_tokens = rows * 16 * 8

    columns = tokens.reshape(rows, 4, 2, 512)
    sent = lax.dynamic_slice_in_dim(columns, 1 - x_hi, 1, 2).reshape(rows, 4 * 512)
    received = over_x_hi(sent)
    tok_other = lax.all_gather(received, "tensor", axis=0, tiled=True, axis_index_groups=CORE_MAJOR)

    left, right = tokens[:, : width // 2], tokens[:, width // 2 :]
    steps = (1, -1, 2)
    beside = over_x_lo(left)
    line = [right, *[over_y(right, step) for step in steps]]
    masked = mask_weights(where, weights, tile_mask, 0, 512, None)
    masked = mask_weights(after(where, received, masked), weights, tile_mask, 512, 1536, masked)
    pair = after(jnp.stack([left, beside]), masked)
    pairs = [pair, *[over_y(pair, step) for step in steps]]
    line = after(jnp.stack(line), masked)
    lines = [line, over_x_lo(line)]
    cot = cotangent.reshape(8, 2, rows, -1).transpose(1, 0, 2, 3).reshape(cotangent.shape)
    masked = mask_weights(after(where, pair, line, cot), weights, tile_mask, 1536, width, masked)
    order = (0, 3, 1, 2)
    here = after(where, masked)
    mine_l = place(here, pairs, [[(0, dy), (1, dy)] for dy in order])
    mine_r = place(here, lines, [[(dx, dy) for dy in order] for dx in range(2)])
    parts = (mine_l, over_core(mine_l), mine_r, over_core(mine_r))

    firsts = [sum(CHUNKS[:i]) for i in range(len(CHUNKS))]
    first, tok = first_grads(where, parts, masked, cot, CHUNKS[0])
    gs, others, got_far, got_near, done = [first], {}, {}, {}, None
    stage = (tok,)

    for items in STAGES:
        finished, previous = [], stage
        for kind, c in items:
            here = after(where, *stage, *previous)
            if kind == "x_hi":
                others[c] = over_x_hi(gs[c])
                finished.append(others[c])
                continue
            if c in others:
                common = (tok, tok_other, gs[c], others[c])
            if kind == "rest":
                gs += rest_grads(here, tok, masked, cot, CHUNKS[0], CHUNKS[1:])
                previous = (gs[1],)
            elif kind == "token":
                share = token_rows(here, gs, masked)
                previous = (share,)
            elif kind == "sum":
                share = after(share, *previous)
                token_grad = lax.psum_scatter(share, "tensor", scatter_dimension=0, tiled=True)
            elif kind == "far":
                up, down = far_rows(here, *common)
                got_far[c] = (over_z(up, 1), over_z(down, -1))
                previous = (up,)
                finished += got_far[c]
            elif kind == "near":
                up, down = near_rows(here, *common, *got_far[c])
                got_near[c] = (over_z(up, 1), over_z(down, -1))
                previous = (up,)
                finished += got_near[c]
            else:
                done = last_rows(
                    here, tile_mask, *common, *got_near[c], weights, scores, firsts[c], done, all_tokens
                )
                previous = (done[0],)
        stage = (*previous, *finished)
    return (token_grad, *done)


def solution(mesh):
    placed = (
        P(("replica", "tensor"), None),
        P("replica", "tensor"),
        P(None, None, "tensor"),
        P("replica", None, "tensor"),
        P(None, None, "tensor"),
    )
    return jax.shard_map(
        shards,
        mesh=mesh,
        in_specs=placed,
        out_specs=(
            P(("replica", "tensor"), None),
            P("replica", None, "tensor"),
            P("replica", None, "tensor"),
        ),
        check_vma=False,
    )
```

```python
import functools
import math

import jax
import jax.numpy as jnp
from jax import lax
from jax.experimental import pallas as pl
from jax.experimental.pallas import tpu as pltpu
from jax.sharding import PartitionSpec as P

TILE = 128
CHUNKS = (2, 2, 2, 1)
CORE_MAJOR = [[*range(0, 16, 2), *range(1, 16, 2)]]
STAGES = (
    (("x_hi", 0), ("rest", 0)),
    (("x_hi", 1), ("far", 0), ("token", 0)),
    (("x_hi", 2), ("near", 0), ("sum", 0), ("far", 1)),
    (("x_hi", 3), ("near", 1), ("far", 2), ("last", 0)),
    (("near", 2), ("far", 3), ("last", 1)),
    (("near", 3), ("last", 2)),
    (("last", 3),),
)
MIB = 1 << 20


def params(mib):
    return pltpu.CompilerParams(vmem_limit_bytes=mib * MIB)


SMALL = pl.CostEstimate(flops=1, bytes_accessed=1, transcendentals=0)


def over_core(v):
    return lax.ppermute(v, "tensor", [(i, i ^ 1) for i in range(16)])


def over_x_lo(v):
    return lax.ppermute(v, "tensor", [(i, i ^ 8) for i in range(16)])


def over_y(v, step):
    pairs = [(i, (i & 9) | (((i >> 1) + step) % 4) << 1) for i in range(16)]
    return lax.ppermute(v, "tensor", pairs)


def over_z(v, step):
    return lax.ppermute(v, "replica", [(i, (i + 2 * step) % 8) for i in range(8)])


def over_x_hi(v):
    return lax.ppermute(v, "replica", [(i, i ^ 1) for i in range(8)])


def after(value, *earlier):
    return lax.optimization_barrier((value, *earlier))[0]


def slot_of(where, dx, dy):
    x_lo = where[2] if dx == 0 else 1 - where[2]
    return x_lo * 4 + lax.rem(where[3] + dy, 4)


def place_body(slots, where, *refs):
    out_ref = refs[-1]
    for piece, group in zip(refs, slots):
        value = piece[...]
        for i, (dx, dy) in enumerate(group):
            out_ref[slot_of(where, dx, dy)] = value[i] if len(group) > 1 else value


def place(where, pieces, slots):
    rows, width = pieces[0].shape[-2:]
    cols = width // 2
    specs = [
        pl.BlockSpec((rows, cols), lambda i, where: (0, i))
        if piece.ndim == 2
        else pl.BlockSpec((piece.shape[0], rows, cols), lambda i, where: (0, 0, i))
        for piece in pieces
    ]
    return pl.pallas_call(
        functools.partial(place_body, slots),
        grid_spec=pltpu.PrefetchScalarGridSpec(
            num_scalar_prefetch=1,
            grid=(2,),
            in_specs=specs,
            out_specs=pl.BlockSpec((8, rows, cols), lambda i, where: (0, 0, i)),
        ),
        out_shape=jax.ShapeDtypeStruct((8, rows, width), jnp.bfloat16),
        compiler_params=params(56),
        cost_estimate=SMALL,
        name="place",
    )(where, *pieces).reshape(8 * rows, width)


def mask_body(tiles, units, begin, where, mask_ref, w_ref, *rest):
    out_ref = rest[-1]
    step = pl.program_id(0) + begin // (tiles * TILE)
    for t in range(tiles):
        rows = slice(t * TILE, (t + 1) * TILE)
        block = w_ref[rows].reshape(TILE, 2 * units * TILE)
        for j in range(units):
            for k in range(2):
                keep = mask_ref[step * tiles + t, k, j].astype(jnp.float32).astype(jnp.bfloat16)
                at = (k * units + j) * TILE
                out_ref[j, rows, k * TILE : (k + 1) * TILE] = block[:, at : at + TILE] * keep


def mask_weights(where, weights, tile_mask, begin, end, done):
    width, pair, hidden = weights.shape
    units = hidden // TILE
    rows = 256
    operands = [where, tile_mask, weights] + ([] if done is None else [done])
    return pl.pallas_call(
        functools.partial(mask_body, rows // TILE, units, begin),
        grid_spec=pltpu.PrefetchScalarGridSpec(
            num_scalar_prefetch=1,
            grid=((end - begin) // rows,),
            in_specs=[
                pl.BlockSpec(memory_space=pltpu.SMEM),
                pl.BlockSpec((rows, pair, hidden), lambda i, where: (i + begin // rows, 0, 0)),
            ]
            + ([] if done is None else [pl.BlockSpec(memory_space=pl.ANY)]),
            out_specs=pl.BlockSpec((units, rows, 256), lambda i, where: (0, i + begin // rows, 0)),
        ),
        out_shape=jax.ShapeDtypeStruct((units, width, 256), jnp.bfloat16),
        input_output_aliases={} if done is None else {3: 0},
        compiler_params=params(56),
        cost_estimate=SMALL,
        name="mask_weights",
    )(*operands)


def unit(tok, w, cot):
    both = jnp.dot(tok, w, preferred_element_type=jnp.float32)
    gate, up = both[:, :TILE], both[:, TILE:]
    sig = 1.0 / (1.0 + jnp.exp(-gate))
    upstream = cot.astype(jnp.float32)
    gate_grad = upstream * up * sig * (1.0 + gate * (1.0 - sig))
    return gate_grad.astype(jnp.bfloat16), (upstream * gate * sig).astype(jnp.bfloat16)


def first_body(where, mine_l, theirs_l, mine_r, theirs_r, w_ref, cot_ref, out_ref, tok_ref, held, sems):
    step = pl.program_id(0)
    saves = [pltpu.make_async_copy(held.at[i], tok_ref.at[i], sems.at[i]) for i in range(2)]

    @pl.when(step == 0)
    def _():
        core = where[4]
        half = mine_l.shape[1]
        left, right = pl.ds(0, half), pl.ds(half, half)
        loads = [
            pltpu.make_async_copy(mine_l, held.at[core, :, left], sems.at[0]),
            pltpu.make_async_copy(theirs_l, held.at[1 - core, :, left], sems.at[1]),
            pltpu.make_async_copy(mine_r, held.at[core, :, right], sems.at[2]),
            pltpu.make_async_copy(theirs_r, held.at[1 - core, :, right], sems.at[3]),
        ]
        for load in loads:
            load.start()
        for load in loads:
            load.wait()
        for save in saves:
            save.start()

    tok = held[...].reshape(2 * held.shape[1], held.shape[2])
    out_ref[0, :, :TILE], out_ref[0, :, TILE:] = unit(tok, w_ref[0], cot_ref[...])

    @pl.when(step == pl.num_programs(0) - 1)
    def _():
        for save in saves:
            save.wait()


def first_grads(where, parts, masked, cot, count):
    rows, width = parts[0].shape[0], masked.shape[1]
    grads, tok = pl.pallas_call(
        first_body,
        grid_spec=pltpu.PrefetchScalarGridSpec(
            num_scalar_prefetch=1,
            grid=(count,),
            in_specs=[
                *[pl.BlockSpec(memory_space=pl.ANY)] * 4,
                pl.BlockSpec((1, width, 256), lambda j, where: (j, 0, 0)),
                pl.BlockSpec((2 * rows, TILE), lambda j, where: (0, j)),
            ],
            out_specs=[
                pl.BlockSpec((1, 2 * rows, 256), lambda j, where: (j, 0, 0)),
                pl.BlockSpec(memory_space=pl.ANY),
            ],
            scratch_shapes=[pltpu.VMEM((2, rows, width), jnp.bfloat16), pltpu.SemaphoreType.DMA((4,))],
        ),
        out_shape=[
            jax.ShapeDtypeStruct((count, 2 * rows, 256), jnp.bfloat16),
            jax.ShapeDtypeStruct((2, rows, width), jnp.bfloat16),
        ],
        compiler_params=params(56),
        cost_estimate=SMALL,
        name="first_grads",
    )(where, *parts, masked, cot)
    return grads, tok.reshape(2 * rows, width)


def rest_body(counts, where, tok_ref, w_ref, cot_ref, *out_refs):
    step = pl.program_id(0)
    gate_grad, up_grad = unit(tok_ref[...], w_ref[0], cot_ref[...])
    start = 0
    for count, out_ref in zip(counts, out_refs):

        @pl.when((step >= start) & (step < start + count))
        def _(out_ref=out_ref):
            out_ref[0, :, :TILE] = gate_grad
            out_ref[0, :, TILE:] = up_grad

        start += count


def rest_grads(where, tok, masked, cot, first, counts):
    rows, width = tok.shape
    n = sum(counts)
    outs, start = [], 0
    for count in counts:
        outs.append(
            pl.BlockSpec(
                (1, rows, 256),
                lambda j, where, s=start, c=count: (jnp.clip(j - s, 0, c - 1), 0, 0),
            )
        )
        start += count
    return pl.pallas_call(
        functools.partial(rest_body, counts),
        grid_spec=pltpu.PrefetchScalarGridSpec(
            num_scalar_prefetch=1,
            grid=(n,),
            in_specs=[
                pl.BlockSpec((rows, width), lambda j, where: (0, 0)),
                pl.BlockSpec((1, width, 256), lambda j, where: (j + first, 0, 0)),
                pl.BlockSpec((rows, TILE), lambda j, where: (0, j + first)),
            ],
            out_specs=outs,
        ),
        out_shape=[jax.ShapeDtypeStruct((c, rows, 256), jnp.bfloat16) for c in counts],
        compiler_params=params(56),
        cost_estimate=SMALL,
        name="rest_grads",
    )(where, tok, masked, cot)


def outer(tok_a, tok_b, g_a, g_b, j):
    dims = (((0,), (0,)), ((), ()))
    return lax.dot_general(
        tok_a[...], g_a[j], dims, preferred_element_type=jnp.float32
    ) + lax.dot_general(tok_b[...], g_b[j], dims, preferred_element_type=jnp.float32)


def far_body(count, where, tok_a, tok_b, g_a, g_b, up_ref, down_ref):
    for j in range(count):
        part = outer(tok_a, tok_b, g_a, g_b, j).astype(jnp.bfloat16)
        up_ref[j] = part[:256]
        down_ref[j] = part[256:]


def near_body(count, where, tok_ua, tok_ub, tok_da, tok_db, g_a, g_b, got_u, got_d, up_ref, down_ref):
    for j in range(count):
        part = outer(tok_ua, tok_ub, g_a, g_b, j)
        up_ref[j, :256] = (part[:256] + got_u[j].astype(jnp.float32)).astype(jnp.bfloat16)
        up_ref[j, 256:] = part[256:].astype(jnp.bfloat16)
        part = outer(tok_da, tok_db, g_a, g_b, j)
        down_ref[j, :256] = part[:256].astype(jnp.bfloat16)
        down_ref[j, 256:] = (part[256:] + got_d[j].astype(jnp.float32)).astype(jnp.bfloat16)


def last_body(
    count, first, scale, rate, where, mask_ref, tok_a, tok_b, g_a, g_b, got_u, got_d, w_ref, s_ref, *rest
):
    wg_ref, ns_ref = rest[-2:]
    row = (where[0] * 2 + where[1]) * 4
    side = lax.broadcasted_iota(jnp.int32, (1, 2, TILE), 1)
    for j in range(count):
        total = outer(tok_a, tok_b, g_a, g_b, j)
        total = total + got_u[j].astype(jnp.float32) + got_d[j].astype(jnp.float32)
        total = total * scale
        cols = slice(j * TILE, (j + 1) * TILE)
        for t in range(4):
            rows = slice(t * TILE, (t + 1) * TILE)
            keep = jnp.where(
                side == 0, mask_ref[row + t, 0, first + j], mask_ref[row + t, 1, first + j]
            ).astype(jnp.float32)
            here = total[rows].reshape(TILE, 2, TILE)
            wg_ref[rows, :, cols] = (here * keep).astype(jnp.bfloat16)
            ns_ref[rows, :, cols] = (
                s_ref[rows, :, cols] - rate * w_ref[rows, :, cols].astype(jnp.float32) * here
            )


def tok_spec(dz):
    return pl.BlockSpec((640, 512), lambda i, where: (0, 2 * ((where[0] + dz) % 4) + where[1]))


def other_spec(dz):
    return pl.BlockSpec((640, 512), lambda i, where: (0, (where[0] + dz) % 4))


def whole(shape):
    return pl.BlockSpec(shape, lambda i, where: (0,) * len(shape))


def far_rows(where, tok, tok_other, g, g_other):
    count = g.shape[0]
    shape = (count, 256, 256)
    return pl.pallas_call(
        functools.partial(far_body, count),
        grid_spec=pltpu.PrefetchScalarGridSpec(
            num_scalar_prefetch=1,
            grid=(1,),
            in_specs=[tok_spec(2), other_spec(2), whole(g.shape), whole(g.shape)],
            out_specs=[whole(shape)] * 2,
        ),
        out_shape=[jax.ShapeDtypeStruct(shape, jnp.bfloat16)] * 2,
        compiler_params=params(56),
        cost_estimate=SMALL,
        name="far_rows",
    )(where, tok, tok_other, g, g_other)


def near_rows(where, tok, tok_other, g, g_other, got_u, got_d):
    count = g.shape[0]
    shape = (count, 512, 256)
    return pl.pallas_call(
        functools.partial(near_body, count),
        grid_spec=pltpu.PrefetchScalarGridSpec(
            num_scalar_prefetch=1,
            grid=(1,),
            in_specs=[
                tok_spec(1),
                other_spec(1),
                tok_spec(3),
                other_spec(3),
                whole(g.shape),
                whole(g.shape),
                whole(got_u.shape),
                whole(got_d.shape),
            ],
            out_specs=[whole(shape)] * 2,
        ),
        out_shape=[jax.ShapeDtypeStruct(shape, jnp.bfloat16)] * 2,
        compiler_params=params(56),
        cost_estimate=SMALL,
        name="near_rows",
    )(where, tok, tok_other, tok, tok_other, g, g_other, got_u, got_d)


def last_rows(where, tile_mask, tok, tok_other, g, g_other, got_u, got_d, weights, scores, first, done, tokens):
    count = g.shape[0]
    n = count * TILE
    at = first // count
    specs = [
        pl.BlockSpec(memory_space=pltpu.SMEM),
        tok_spec(0),
        other_spec(0),
        whole(g.shape),
        whole(g.shape),
        whole(got_u.shape),
        whole(got_d.shape),
        pl.BlockSpec((512, 2, n), lambda i, where: (where[0] * 2 + where[1], 0, at)),
        pl.BlockSpec((512, 2, n), lambda i, where: (0, 0, at)),
    ]
    out = pl.BlockSpec((512, 2, n), lambda i, where: (0, 0, at))
    operands = [where, tile_mask, tok, tok_other, g, g_other, got_u, got_d, weights, scores]
    alias = {}
    if done is not None:
        alias = {len(operands): 0, len(operands) + 1: 1}
        specs += [pl.BlockSpec(memory_space=pl.ANY)] * 2
        operands += list(done)
    return pl.pallas_call(
        functools.partial(last_body, count, first, 1.0 / math.sqrt(tokens), math.sqrt(weights.shape[0])),
        grid_spec=pltpu.PrefetchScalarGridSpec(
            num_scalar_prefetch=1, grid=(1,), in_specs=specs, out_specs=[out, out]
        ),
        out_shape=[
            jax.ShapeDtypeStruct(scores.shape, jnp.bfloat16),
            jax.ShapeDtypeStruct(scores.shape, jnp.float32),
        ],
        input_output_aliases=alias,
        compiler_params=params(56),
        cost_estimate=SMALL,
        name="last_rows",
    )(*operands)


def token_body(parts, where, *refs):
    w_ref, out_ref = refs[parts:]
    total = None
    at = 0
    for g in refs[:parts]:
        for j in range(g.shape[0]):
            term = lax.dot_general(
                g[j], w_ref[at], (((1,), (1,)), ((), ())), preferred_element_type=jnp.float32
            )
            total = term if total is None else total + term
            at += 1
    rows = out_ref.shape[1]
    for i in range(8):
        for core in range(2):
            start = (core * 8 + i) * rows
            out_ref[i * 2 + core] = total[start : start + rows].astype(jnp.bfloat16)


def token_rows(where, gs, masked):
    units, width, unused = masked.shape
    rows, cols = gs[0].shape[1], 512
    specs = [pl.BlockSpec(g.shape, lambda i, where: (0, 0, 0)) for g in gs]
    specs.append(pl.BlockSpec((units, cols, 256), lambda i, where: (0, i, 0)))
    return pl.pallas_call(
        functools.partial(token_body, len(gs)),
        grid_spec=pltpu.PrefetchScalarGridSpec(
            num_scalar_prefetch=1,
            grid=(width // cols,),
            in_specs=specs,
            out_specs=pl.BlockSpec((16, rows // 16, cols), lambda i, where: (0, 0, i)),
        ),
        out_shape=jax.ShapeDtypeStruct((16, rows // 16, width), jnp.bfloat16),
        compiler_params=params(56),
        cost_estimate=SMALL,
        name="token_rows",
    )(where, *gs, masked).reshape(rows, width)


def shards(tokens, cotangent, weights, scores, tile_mask):
    place_at, replica = lax.axis_index("tensor"), lax.axis_index("replica")
    z, x_hi = replica // 2, replica % 2
    where = jnp.stack([z, x_hi, place_at // 8, (place_at // 2) % 4, place_at % 2]).astype(jnp.int32)
    rows, width = tokens.shape
    all_tokens = rows * 16 * 8

    columns = tokens.reshape(rows, 4, 2, 512)
    sent = lax.dynamic_slice_in_dim(columns, 1 - x_hi, 1, 2).reshape(rows, 4 * 512)
    received = over_x_hi(sent)
    tok_other = lax.all_gather(received, "tensor", axis=0, tiled=True, axis_index_groups=CORE_MAJOR)

    left, right = tokens[:, : width // 2], tokens[:, width // 2 :]
    steps = (1, -1, 2)
    beside = over_x_lo(left)
    line = [right, *[over_y(right, step) for step in steps]]
    masked = mask_weights(after(where, received), weights, tile_mask, 0, 768, None)
    pair = after(jnp.stack([left, beside]), masked)
    pairs = [pair, *[over_y(pair, step) for step in steps]]
    line = after(jnp.stack(line), masked)
    lines = [line, over_x_lo(line)]
    cot = cotangent.reshape(8, 2, rows, -1).transpose(1, 0, 2, 3).reshape(cotangent.shape)
    masked = mask_weights(after(where, pair, line, cot), weights, tile_mask, 768, width, masked)
    order = (0, 3, 1, 2)
    here = after(where, masked)
    mine_l = place(here, pairs, [[(0, dy), (1, dy)] for dy in order])
    mine_r = place(here, lines, [[(dx, dy) for dy in order] for dx in range(2)])
    parts = (mine_l, over_core(mine_l), mine_r, over_core(mine_r))

    firsts = [sum(CHUNKS[:i]) for i in range(len(CHUNKS))]
    first, tok = first_grads(where, parts, masked, cot, CHUNKS[0])
    gs, others, got_far, got_near, done = [first], {}, {}, {}, None
    stage = (tok,)

    for items in STAGES:
        finished, previous = [], stage
        for kind, c in items:
            here = after(where, *stage, *previous)
            if kind == "x_hi":
                others[c] = over_x_hi(gs[c])
                finished.append(others[c])
                continue
            if c in others:
                common = (tok, tok_other, gs[c], others[c])
            if kind == "rest":
                gs += rest_grads(here, tok, masked, cot, CHUNKS[0], CHUNKS[1:])
                previous = (gs[1],)
            elif kind == "token":
                share = token_rows(here, gs, masked)
                previous = (share,)
            elif kind == "sum":
                share = after(share, *previous)
                token_grad = lax.psum_scatter(share, "tensor", scatter_dimension=0, tiled=True)
            elif kind == "far":
                up, down = far_rows(here, *common)
                got_far[c] = (over_z(up, 1), over_z(down, -1))
                previous = (up,)
                finished += got_far[c]
            elif kind == "near":
                up, down = near_rows(here, *common, *got_far[c])
                got_near[c] = (over_z(up, 1), over_z(down, -1))
                previous = (up,)
                finished += got_near[c]
            else:
                done = last_rows(
                    here, tile_mask, *common, *got_near[c], weights, scores, firsts[c], done, all_tokens
                )
                previous = (done[0],)
        stage = (*previous, *finished)
    return (token_grad, *done)


def solution(mesh):
    placed = (
        P(("replica", "tensor"), None),
        P("replica", "tensor"),
        P(None, None, "tensor"),
        P("replica", None, "tensor"),
        P(None, None, "tensor"),
    )
    return jax.shard_map(
        shards,
        mesh=mesh,
        in_specs=placed,
        out_specs=(
            P(("replica", "tensor"), None),
            P("replica", None, "tensor"),
            P("replica", None, "tensor"),
        ),
        check_vma=False,
    )
```
